512 devices in a mesh: row: 16 (over y, core), col: 32 (over z, x).
Axes of the slice: x: 4, y: 8, z: 8, core: 2. Of those that a mesh axis runs over, the one named last changes fastest.
Arguments:
- features: bfloat16 [65536, 256], P(('col', 'row')), may hold values from -6 to 6
- col_norm: float32 [65536], P(('col', 'row')), may hold values from 0.03 to 0.3
- weight: bfloat16 [256, 256], replicated, may hold values from -0.375 to 0.375
- bias: float32 [256], replicated, may hold values from -4 to 4
- tile_coords: int32 [16, 32, 24, 2], P('row', 'col'), may hold values from 0 to 31, as said below
- tile_count: int32 [16, 32], P('row', 'col'), may hold values from 6 to 24
- tile_values: bfloat16 [16, 32, 24, 128, 128], P('row', 'col'), may hold values from 0 to 1
- row_norm: float32 [65536], P(('row', 'col')), may hold values from 0.03 to 0.3
- cotangent: bfloat16 [65536, 256], P(('row', 'col')), may hold values from -6 to 6
Outputs:
- output: bfloat16 [65536, 256], P(('row', 'col'))
- grad_features: bfloat16 [65536, 256], P(('col', 'row'))
- grad_weight: float32 [256, 256], replicated
- grad_bias: float32 [256], replicated
The draws below stay inside these ranges and needn't reach their ends.
Inputs may be any that keep to these rules, and one draw needn't show every extreme that they name: `tile_coords`: column 0 is a tile row below 32, column 1 a tile column below 16; the 24 pairs of one grid block are distinct. Slots from tile_count onward hold no tiles.
All inputs are finite; a program needn't handle non-finite values.
Results may differ from the reference program's by a relative error of at most 0.025.
Values may be sent and summed in bfloat16 or wider, within the bound.
No kernel may reach another device: no remote copies, remote signals or barrier semaphores. Data moves between devices by JAX's collectives and lax.ppermute only.
A program may use at most 64 MiB of HBM per device.

```python
import math
import jax
import jax.numpy as jnp
from jax import lax

HIDDEN_SIZE = 256
TILE_SIZE = 128
TILE_COLS = 16
TILE_SLOTS = 24
TILE_ROWS = 32
NODE_COUNT = 65536
N_ROW = 16
N_COL = 32


def draw_tile_coords(key, part):
    key = jax.random.fold_in(key, 11)
    blocks = N_ROW * N_COL
    places = TILE_ROWS * TILE_COLS
    keys = jax.random.split(key, blocks)

    def one_block(block_key):
        first_key, second_key = jax.random.split(block_key)
        order = jax.random.permutation(first_key, places).astype(jnp.int32)
        corner = places - 1
        where = jnp.argmax(order == corner)
        target = jax.random.randint(second_key, (), 0, TILE_SLOTS // 4)
        moved = order[target]
        order = order.at[where].set(moved)
        order = order.at[target].set(corner)
        chosen = order[:TILE_SLOTS]
        return jnp.stack([chosen // TILE_COLS, chosen % TILE_COLS], axis=-1)
    result = jax.vmap(one_block)(keys)
    return result.reshape(N_ROW, N_COL, TILE_SLOTS, 2).astype(jnp.int32)


def draw_tile_count(key, part):
    key = jax.random.fold_in(key, 23)
    first_key, second_key = jax.random.split(key)
    lowest = TILE_SLOTS // 4
    uniform_part = jax.random.randint(first_key, (N_ROW * N_COL,), 0, TILE_SLOTS + 1)
    counts = lowest + (TILE_SLOTS - lowest) * uniform_part * uniform_part // (TILE_SLOTS * TILE_SLOTS)
    fullest = jax.random.randint(second_key, (), 0, N_ROW * N_COL)
    counts = counts.at[fullest].set(TILE_SLOTS)
    return counts.reshape(N_ROW, N_COL).astype(jnp.int32)


def level_of(stream_key, shape, cuts, smallest, high):
    gain = 1.0
    for dim, blocks in cuts:
        steps = jax.random.uniform(jax.random.fold_in(jax.random.fold_in(stream_key, 6), dim), (blocks,), jnp.float32, smallest / len(cuts), high / len(cuts))
        gain = gain * jnp.repeat(jnp.exp(steps), shape[dim] // blocks).reshape((-1,) + (1,) * (len(shape) - 1 - dim))
    return gain


def bell_draw(key, shape, deviation, reach, cuts=(), dtype=jnp.bfloat16):
    drawn = deviation * jax.random.normal(key, shape, jnp.float32)
    if cuts:
        drawn = drawn * level_of(key, shape, cuts, -0.22, 0.18)
    return jnp.clip(drawn, -reach, reach).astype(dtype)


def setup_inputs(seed: int = 0) -> dict:
    key_list = jax.random.split(jax.random.key(seed), 10)
    features = bell_draw(key_list[0], (NODE_COUNT, HIDDEN_SIZE), 1.0, 6.0, ((0, 512),))
    col_norm = jnp.clip(jnp.exp(math.log(0.3) - 2.3025852 * jax.random.uniform(key_list[1], (NODE_COUNT,), jnp.float32) ** level_of(key_list[1], (NODE_COUNT,), ((0, 512),), -0.2, 0.2)), 0.03, 0.3)
    weight = bell_draw(key_list[2], (HIDDEN_SIZE, HIDDEN_SIZE), HIDDEN_SIZE ** -0.5, 0.375)
    bias = bell_draw(key_list[3], (HIDDEN_SIZE,), 1.0, 4.0, (), jnp.float32)
    tile_coords = draw_tile_coords(jax.random.fold_in(key_list[9], 71), 0)
    tile_count = draw_tile_count(jax.random.fold_in(key_list[9], 71), 0)
    tile_values = jnp.clip(1.0 * jax.random.uniform(key_list[6], (N_ROW, N_COL, TILE_SLOTS, TILE_SIZE, TILE_SIZE), jnp.float32) ** level_of(key_list[6], (N_ROW, N_COL, TILE_SLOTS, TILE_SIZE, TILE_SIZE), ((0, 16), (1, 32)), -0.2, 0.2), 0.0, 1.0).astype(jnp.bfloat16)
    row_norm = jnp.clip(jnp.exp(math.log(0.3) - 2.3025852 * jax.random.uniform(key_list[7], (NODE_COUNT,), jnp.float32) ** level_of(key_list[7], (NODE_COUNT,), ((0, 512),), -0.2, 0.2)), 0.03, 0.3)
    cotangent = bell_draw(key_list[8], (NODE_COUNT, HIDDEN_SIZE), 1.0, 6.0, ((0, 512),))
    return dict(features=features, col_norm=col_norm, weight=weight, bias=bias, tile_coords=tile_coords, tile_count=tile_count, tile_values=tile_values, row_norm=row_norm, cotangent=cotangent)


def reference(features, col_norm, weight, bias, tile_coords, tile_count, tile_values, row_norm, cotangent):
    highest = lax.Precision.HIGHEST
    block_rows = TILE_ROWS * TILE_SIZE
    block_cols = TILE_COLS * TILE_SIZE
    mixed = jnp.dot(features, weight, preferred_element_type=jnp.float32)
    panel_all = (col_norm[:, None] * mixed).astype(jnp.bfloat16)
    live = jnp.arange(TILE_SLOTS)[None, None, :] < tile_count[:, :, None]
    row_pick = jnp.logical_and(tile_coords[..., 0][..., None] == jnp.arange(TILE_ROWS)[None, None, None, :], live[..., None]).astype(jnp.float32)
    col_pick = jnp.logical_and(tile_coords[..., 1][..., None] == jnp.arange(TILE_COLS)[None, None, None, :], live[..., None]).astype(jnp.float32)
    row_ids = jnp.arange(N_ROW).astype(jnp.int32)
    col_ids = jnp.arange(N_COL).astype(jnp.int32)

    def forward_row(i):
        def step(total, j):
            start = (j * block_cols).astype(jnp.int32)
            panel = lax.dynamic_slice_in_dim(panel_all, start, block_cols, 0).reshape(TILE_COLS, TILE_SIZE, HIDDEN_SIZE)
            picked = panel[tile_coords[i, j, :, 1]].astype(jnp.float32)
            product = jnp.einsum("kab,kbh->kah", tile_values[i, j].astype(jnp.float32), picked, precision=highest)
            term = jnp.einsum("kr,kah->rah", row_pick[i, j], product, precision=highest).reshape(block_rows, HIDDEN_SIZE)
            rounded = lax.optimization_barrier(term.astype(jnp.bfloat16))
            return total + rounded.astype(jnp.float32), None

        total, unused = lax.scan(step, jnp.zeros((block_rows, HIDDEN_SIZE), jnp.float32), col_ids)
        return total

    rowsum = lax.map(forward_row, row_ids).reshape(NODE_COUNT, HIDDEN_SIZE)
    pre = row_norm[:, None] * rowsum + bias[None, :]
    sigma = jax.nn.sigmoid(pre)
    output = (pre * sigma).astype(jnp.bfloat16)
    grad_pre = cotangent.astype(jnp.float32) * (sigma * (1.0 + pre * (1.0 - sigma)))
    grad_rows = (grad_pre * row_norm[:, None]).astype(jnp.bfloat16)

    def backward_col(j):
        def step(total, i):
            start = (i * block_rows).astype(jnp.int32)
            rows = lax.dynamic_slice_in_dim(grad_rows, start, block_rows, 0).reshape(TILE_ROWS, TILE_SIZE, HIDDEN_SIZE)
            picked = rows[tile_coords[i, j, :, 0]].astype(jnp.float32)
            product = jnp.einsum("kba,kbh->kah", tile_values[i, j].astype(jnp.float32), picked, precision=highest)
            term = jnp.einsum("kc,kah->cah", col_pick[i, j], product, precision=highest).reshape(block_cols, HIDDEN_SIZE)
            rounded = lax.optimization_barrier(term.astype(jnp.bfloat16))
            return total + rounded.astype(jnp.float32), None

        total, unused = lax.scan(step, jnp.zeros((block_cols, HIDDEN_SIZE), jnp.float32), row_ids)
        return total

    colsum = lax.map(backward_col, col_ids).reshape(NODE_COUNT, HIDDEN_SIZE)
    grad_mixed = (col_norm[:, None] * colsum).astype(jnp.bfloat16)
    grad_features = jnp.dot(grad_mixed, weight.T, preferred_element_type=jnp.float32).astype(jnp.bfloat16)
    scale = float(NODE_COUNT) ** -0.5
    grad_weight = jnp.dot(features.T, grad_mixed, preferred_element_type=jnp.float32) * scale
    grad_bias = jnp.sum(grad_pre, axis=0) * scale
    return (output, grad_features, grad_weight, grad_bias)
```

```python
import jax
import jax.numpy as jnp
from jax import lax
from jax.experimental import pallas as pl
from jax.experimental.pallas import tpu as pltpu
from jax.sharding import Mesh, PartitionSpec as P

COL = ("z", "x")
ROW = ("y", "core")
VMEM = pl.BlockSpec(memory_space=pltpu.VMEM)
SMEM = pl.BlockSpec(memory_space=pltpu.SMEM)
F32 = jnp.float32
BF16 = jnp.bfloat16


def forward_kernel(info, tiles, own, other, out, total):
    slots = tiles.shape[0]
    core = info[2 * slots + 1]
    total[...] = jnp.zeros_like(total)

    def step(k, _):
        r = info[k]
        c = info[slots + k]
        half = c // 2
        mine = (c % 2) == core
        picked = jnp.where(mine, own[half], other[half])
        total[r] += jnp.dot(tiles[k], picked, preferred_element_type=F32)
        return 0

    lax.fori_loop(0, info[2 * slots], step, 0)
    out[...] = total[...].astype(out.dtype)


def backward_kernel(info, tiles, g0, g1, g2, g3, keep, send, total):
    slots = tiles.shape[0]
    core = info[2 * slots + 1]
    here = info[2 * slots + 2]
    n_half = keep.shape[0]
    total[...] = jnp.zeros_like(total)

    def step(k, _):
        r = info[k]
        c = info[slots + k]
        z = r // 4
        d = (r % 4 - here + 4) % 4
        picked = jnp.where(
            d < 2,
            jnp.where(d == 0, g0[z], g1[z]),
            jnp.where(d == 2, g2[z], g3[z]),
        )
        place = jnp.where((c % 2) == core, 0, n_half) + c // 2
        total[place] += lax.dot_general(
            tiles[k], picked, (((0,), (0,)), ((), ())), preferred_element_type=F32
        )
        return 0

    lax.fori_loop(0, info[2 * slots], step, 0)
    keep[...] = total[:n_half]
    send[...] = total[n_half:].astype(send.dtype)


def repeat(a, n):
    return jnp.broadcast_to(a[None], (n,) + a.shape)


def body(
    features, col_norm, weight, bias, tile_coords, tile_count, tile_values, row_norm, cotangent
):
    n, hidden = features.shape
    n_y, n_core = lax.axis_size("y"), lax.axis_size("core")
    n_z, n_x = lax.axis_size("z"), lax.axis_size("x")
    tile_rows, tile_cols = n_z * n_x, n_y * n_core
    scale = float(n * tile_rows * tile_cols) ** (-0.5)
    tiles = tile_values[0, 0]
    coords = tile_coords[0, 0]
    swap = [(0, 1), (1, 0)]
    info = jnp.concatenate(
        [
            coords[:, 0],
            coords[:, 1],
            tile_count[0],
            lax.axis_index("core").reshape(1),
            lax.axis_index("x").reshape(1),
        ]
    )

    share = (col_norm[:, None] * features.astype(F32)).astype(BF16)
    own = lax.all_to_all(repeat(share, n_y), "y", 0, 0, tiled=True)
    other = lax.ppermute(own, "core", swap)

    part = hidden // 2
    sums = []
    for h in range(2):
        block = pl.pallas_call(
            forward_kernel,
            out_shape=jax.ShapeDtypeStruct((tile_rows, n, part), BF16),
            in_specs=[SMEM, VMEM, VMEM, VMEM],
            out_specs=VMEM,
            scratch_shapes=[pltpu.VMEM((tile_rows, n, part), F32)],
            compiler_params=pltpu.CompilerParams(vmem_limit_bytes=40 * 2**20),
            name="forward_tiles",
        )(info, tiles, own[:, :, h * part : (h + 1) * part], other[:, :, h * part : (h + 1) * part])
        terms = lax.all_to_all(block, COL, 0, 0, tiled=True)
        sums.append(jnp.sum(terms.astype(F32), axis=0))
    mixed = jnp.concatenate(sums, axis=1)

    high = mixed.astype(BF16)
    low = (mixed - high.astype(F32)).astype(BF16)
    rowsum = jnp.dot(high, weight, preferred_element_type=F32) + jnp.dot(
        low, weight, preferred_element_type=F32
    )
    pre = row_norm[:, None] * rowsum + bias[None, :]
    sigma = jax.nn.sigmoid(pre)
    output = (pre * sigma).astype(BF16)
    grad_pre = cotangent.astype(F32) * (sigma * (1.0 + pre * (1.0 - sigma)))
    grad_here = (grad_pre * row_norm[:, None]).astype(BF16)

    g0 = lax.all_to_all(repeat(grad_here, n_z), "z", 0, 0, tiled=True)
    g = [g0]
    for d in range(1, n_x):
        g.append(lax.ppermute(g0, "x", [((i + d) % n_x, i) for i in range(n_x)]))

    weight_part = lax.dot_general(
        high, grad_here, (((0,), (0,)), ((), ())), preferred_element_type=F32
    )
    bias_part = jnp.sum(grad_pre, axis=0)
    both = jnp.concatenate(
        [weight_part, jnp.broadcast_to(bias_part[:, None], (hidden, 128))], axis=1
    )
    both = (both * scale).reshape(tile_rows, hidden // tile_rows, hidden + 128)
    both = jnp.sum(lax.all_to_all(both, COL, 0, 0, tiled=True), axis=0)
    both = jnp.sum(lax.all_to_all(repeat(both, tile_cols), ROW, 0, 0, tiled=True), axis=0)
    both = lax.all_to_all(repeat(both, tile_rows), COL, 0, 0, tiled=True)
    both = both.reshape(hidden, hidden + 128)
    grad_weight = both[:, :hidden]
    grad_bias = both[:, hidden]

    keep, send = pl.pallas_call(
        backward_kernel,
        out_shape=(
            jax.ShapeDtypeStruct((n_y, n, hidden), F32),
            jax.ShapeDtypeStruct((n_y, n, hidden), BF16),
        ),
        in_specs=[SMEM, VMEM, VMEM, VMEM, VMEM, VMEM],
        out_specs=(VMEM, VMEM),
        scratch_shapes=[pltpu.VMEM((tile_cols, n, hidden), F32)],
        compiler_params=pltpu.CompilerParams(vmem_limit_bytes=40 * 2**20),
        name="backward_tiles",
    )(info, tiles, *g)
    pair = (keep + lax.ppermute(send, "core", swap).astype(F32)).astype(BF16)
    column_total = jnp.sum(lax.all_to_all(pair, "y", 0, 0, tiled=True).astype(F32), axis=0)
    grad_mixed = (col_norm[:, None] * column_total).astype(BF16)
    grad_features = lax.dot_general(
        grad_mixed, weight, (((1,), (1,)), ((), ())), preferred_element_type=F32
    ).astype(BF16)
    return (output, grad_features, grad_weight, grad_bias)


def solution(mesh):
    devices = mesh.devices
    sub = Mesh(devices.reshape(8, 2, 8, 4), ("y", "core", "z", "x"))
    by_col = ("z", "x", "y", "core")
    by_row = ("y", "core", "z", "x")
    in_specs = (
        P(by_col, None),
        P(by_col),
        P(),
        P(),
        P(ROW, COL, None, None),
        P(ROW, COL),
        P(ROW, COL, None, None, None),
        P(by_row),
        P(by_row, None),
    )
    out_specs = (P(by_row, None), P(by_col, None), P(), P())
    return jax.shard_map(body, mesh=sub, in_specs=in_specs, out_specs=out_specs, check_vma=False)
```

```python
import jax
import jax.numpy as jnp
from jax import lax
from jax.experimental import pallas as pl
from jax.experimental.pallas import tpu as pltpu
from jax.sharding import Mesh, PartitionSpec as P

COL = ("z", "x")
ROW = ("y", "core")
VMEM = pl.BlockSpec(memory_space=pltpu.VMEM)
SMEM = pl.BlockSpec(memory_space=pltpu.SMEM)
F32 = jnp.float32
BF16 = jnp.bfloat16


UNROLL = 4


def forward_kernel(info, tiles, own, other, o0, o1, o2, o3, total):
    slots = tiles.shape[0]
    count = info[2 * slots]
    core = info[2 * slots + 1]
    here = info[2 * slots + 2]
    n_x, n_z = 4, o0.shape[0]
    total[...] = jnp.zeros_like(total)

    def step(b, _):
        places, products = [], []
        for u in range(UNROLL):
            k = b * UNROLL + u
            r = info[k]
            c = info[slots + k]
            half = c // 2
            picked = jnp.where((c % 2) == core, own[half], other[half])
            product = jnp.dot(tiles[k], picked, preferred_element_type=F32)
            products.append(jnp.where(k < count, product, 0.0))
            places.append((r % n_x - here + n_x) % n_x * n_z + r // n_x)
        for place, product in zip(places, products):
            total[place] += product
        return 0

    lax.fori_loop(0, (count + UNROLL - 1) // UNROLL, step, 0)
    for d, out in enumerate((o0, o1, o2, o3)):
        out[...] = total[d * n_z : (d + 1) * n_z].astype(out.dtype)


def backward_kernel(info, tiles, g0, g1, g2, g3, keep, send, total):
    slots = tiles.shape[0]
    count = info[2 * slots]
    core = info[2 * slots + 1]
    here = info[2 * slots + 2]
    n_half = keep.shape[0]
    total[...] = jnp.zeros_like(total)

    def step(b, _):
        places, products = [], []
        for u in range(UNROLL):
            k = b * UNROLL + u
            r = info[k]
            c = info[slots + k]
            z = r // 4
            d = (r % 4 - here + 4) % 4
            picked = jnp.where(
                d < 2,
                jnp.where(d == 0, g0[z], g1[z]),
                jnp.where(d == 2, g2[z], g3[z]),
            )
            product = lax.dot_general(
                tiles[k], picked, (((0,), (0,)), ((), ())), preferred_element_type=F32
            )
            products.append(jnp.where(k < count, product, 0.0))
            places.append(jnp.where((c % 2) == core, 0, n_half) + c // 2)
        for place, product in zip(places, products):
            total[place] += product
        return 0

    lax.fori_loop(0, (count + UNROLL - 1) // UNROLL, step, 0)
    keep[...] = total[:n_half]
    send[...] = total[n_half:].astype(send.dtype)


def ring(n, d):
    return [(i, (i + d) % n) for i in range(n)]


def repeat(a, n):
    return jnp.broadcast_to(a[None], (n,) + a.shape)


def body(
    features, col_norm, weight, bias, tile_coords, tile_count, tile_values, row_norm, cotangent
):
    n, hidden = features.shape
    n_y, n_core = lax.axis_size("y"), lax.axis_size("core")
    n_z, n_x = lax.axis_size("z"), lax.axis_size("x")
    tile_rows, tile_cols = n_z * n_x, n_y * n_core
    scale = float(n * tile_rows * tile_cols) ** (-0.5)
    tiles = tile_values[0, 0]
    coords = tile_coords[0, 0]
    swap = [(0, 1), (1, 0)]
    info = jnp.concatenate(
        [
            coords[:, 0],
            coords[:, 1],
            tile_count[0],
            lax.axis_index("core").reshape(1),
            lax.axis_index("x").reshape(1),
        ]
    )

    share = (col_norm[:, None] * features.astype(F32)).astype(BF16)
    own = lax.all_to_all(repeat(share, n_y), "y", 0, 0, tiled=True)
    other = lax.ppermute(own, "core", swap)

    part = hidden // 2
    sums = []
    for h in range(2):
        cut = slice(h * part, (h + 1) * part)
        blocks = pl.pallas_call(
            forward_kernel,
            out_shape=(jax.ShapeDtypeStruct((n_z, n, part), BF16),) * n_x,
            in_specs=[SMEM, VMEM, VMEM, VMEM],
            out_specs=(VMEM,) * n_x,
            scratch_shapes=[pltpu.VMEM((tile_rows, n, part), F32)],
            compiler_params=pltpu.CompilerParams(vmem_limit_bytes=40 * 2**20),
            name="forward_tiles",
        )(info, tiles, own[:, :, cut], other[:, :, cut])
        over_x = blocks[0].astype(F32)
        for d in range(1, n_x):
            over_x += lax.ppermute(blocks[d], "x", ring(n_x, d)).astype(F32)
        terms = lax.all_to_all(over_x.astype(BF16), "z", 0, 0, tiled=True)
        sums.append(jnp.sum(terms.astype(F32), axis=0))
    mixed = jnp.concatenate(sums, axis=1)

    high = mixed.astype(BF16)
    low = (mixed - high.astype(F32)).astype(BF16)
    rowsum = jnp.dot(high, weight, preferred_element_type=F32) + jnp.dot(
        low, weight, preferred_element_type=F32
    )
    pre = row_norm[:, None] * rowsum + bias[None, :]
    sigma = jax.nn.sigmoid(pre)
    output = (pre * sigma).astype(BF16)
    grad_pre = cotangent.astype(F32) * (sigma * (1.0 + pre * (1.0 - sigma)))
    grad_here = (grad_pre * row_norm[:, None]).astype(BF16)

    g0 = lax.all_to_all(repeat(grad_here, n_z), "z", 0, 0, tiled=True)
    g = [g0]
    for d in range(1, n_x):
        g.append(lax.ppermute(g0, "x", [((i + d) % n_x, i) for i in range(n_x)]))

    weight_part = lax.dot_general(
        high, grad_here, (((0,), (0,)), ((), ())), preferred_element_type=F32
    )
    bias_part = jnp.sum(grad_pre, axis=0)
    both = jnp.concatenate(
        [weight_part, jnp.broadcast_to(bias_part[:, None], (hidden, 128))], axis=1
    )
    both = (both * scale).reshape(tile_rows, hidden // tile_rows, hidden + 128)
    both = jnp.sum(lax.all_to_all(both, COL, 0, 0, tiled=True), axis=0)
    both = jnp.sum(lax.all_to_all(repeat(both, tile_cols), ROW, 0, 0, tiled=True), axis=0)
    both = lax.all_to_all(repeat(both, tile_rows), COL, 0, 0, tiled=True)
    both = both.reshape(hidden, hidden + 128)
    grad_weight = both[:, :hidden]
    grad_bias = both[:, hidden]

    keep, send = pl.pallas_call(
        backward_kernel,
        out_shape=(
            jax.ShapeDtypeStruct((n_y, n, hidden), F32),
            jax.ShapeDtypeStruct((n_y, n, hidden), BF16),
        ),
        in_specs=[SMEM, VMEM, VMEM, VMEM, VMEM, VMEM],
        out_specs=(VMEM, VMEM),
        scratch_shapes=[pltpu.VMEM((tile_cols, n, hidden), F32)],
        compiler_params=pltpu.CompilerParams(vmem_limit_bytes=40 * 2**20),
        name="backward_tiles",
    )(info, tiles, *g)
    pair = (keep + lax.ppermute(send, "core", swap).astype(F32)).astype(BF16)
    column_total = jnp.sum(lax.all_to_all(pair, "y", 0, 0, tiled=True).astype(F32), axis=0)
    grad_mixed = (col_norm[:, None] * column_total).astype(BF16)
    grad_features = lax.dot_general(
        grad_mixed, weight, (((1,), (1,)), ((), ())), preferred_element_type=F32
    ).astype(BF16)
    return (output, grad_features, grad_weight, grad_bias)


def solution(mesh):
    devices = mesh.devices
    sub = Mesh(devices.reshape(8, 2, 8, 4), ("y", "core", "z", "x"))
    by_col = ("z", "x", "y", "core")
    by_row = ("y", "core", "z", "x")
    in_specs = (
        P(by_col, None),
        P(by_col),
        P(),
        P(),
        P(ROW, COL, None, None),
        P(ROW, COL),
        P(ROW, COL, None, None, None),
        P(by_row),
        P(by_row, None),
    )
    out_specs = (P(by_row, None), P(by_col, None), P(), P())
    return jax.shard_map(body, mesh=sub, in_specs=in_specs, out_specs=out_specs, check_vma=False)
```

```python
import jax
import jax.numpy as jnp
from jax import lax
from jax.experimental import pallas as pl
from jax.experimental.pallas import tpu as pltpu
from jax.sharding import Mesh, PartitionSpec as P

COL = ("z", "x")
ROW = ("y", "core")
VMEM = pl.BlockSpec(memory_space=pltpu.VMEM)
SMEM = pl.BlockSpec(memory_space=pltpu.SMEM)
F32 = jnp.float32
BF16 = jnp.bfloat16


UNROLL = 4


def forward_kernel(info, tiles, own, other, o0, o1, o2, o3, total):
    slots = tiles.shape[0]
    count = info[2 * slots]
    core = info[2 * slots + 1]
    here = info[2 * slots + 2]
    n_x, n_z = 4, o0.shape[0]
    total[...] = jnp.zeros_like(total)

    def step(b, _):
        places, products = [], []
        for u in range(UNROLL):
            k = b * UNROLL + u
            r = info[k]
            c = info[slots + k]
            half = c // 2
            picked = jnp.where((c % 2) == core, own[half], other[half])
            product = jnp.dot(tiles[k], picked, preferred_element_type=F32)
            products.append(jnp.where(k < count, product, 0.0))
            places.append((r % n_x - here + n_x) % n_x * n_z + r // n_x)
        for place, product in zip(places, products):
            total[place] += product
        return 0

    lax.fori_loop(0, (count + UNROLL - 1) // UNROLL, step, 0)
    for d, out in enumerate((o0, o1, o2, o3)):
        out[...] = total[d * n_z : (d + 1) * n_z].astype(out.dtype)


def backward_kernel(info, tiles, g0, g1, g2, g3, keep, send, total):
    slots = tiles.shape[0]
    count = info[2 * slots]
    core = info[2 * slots + 1]
    here = info[2 * slots + 2]
    n_half = keep.shape[0]
    total[...] = jnp.zeros_like(total)

    def step(b, _):
        places, products = [], []
        for u in range(UNROLL):
            k = b * UNROLL + u
            r = info[k]
            c = info[slots + k]
            z = r // 4
            d = (r % 4 - here + 4) % 4
            picked = jnp.where(
                d < 2,
                jnp.where(d == 0, g0[z], g1[z]),
                jnp.where(d == 2, g2[z], g3[z]),
            )
            product = lax.dot_general(
                tiles[k], picked, (((0,), (0,)), ((), ())), preferred_element_type=F32
            )
            products.append(jnp.where(k < count, product, 0.0))
            places.append(jnp.where((c % 2) == core, 0, n_half) + c // 2)
        for place, product in zip(places, products):
            total[place] += product
        return 0

    lax.fori_loop(0, (count + UNROLL - 1) // UNROLL, step, 0)
    keep[...] = total[:n_half]
    send[...] = total[n_half:].astype(send.dtype)


def ring(n, d):
    return [(i, (i + d) % n) for i in range(n)]


def repeat(a, n):
    return jnp.broadcast_to(a[None], (n,) + a.shape)


def body(
    features, col_norm, weight, bias, tile_coords, tile_count, tile_values, row_norm, cotangent
):
    n, hidden = features.shape
    n_y, n_core = lax.axis_size("y"), lax.axis_size("core")
    n_z, n_x = lax.axis_size("z"), lax.axis_size("x")
    tile_rows, tile_cols = n_z * n_x, n_y * n_core
    scale = float(n * tile_rows * tile_cols) ** (-0.5)
    tiles = tile_values[0, 0]
    coords = tile_coords[0, 0]
    swap = [(0, 1), (1, 0)]
    info = jnp.concatenate(
        [
            coords[:, 0],
            coords[:, 1],
            tile_count[0],
            lax.axis_index("core").reshape(1),
            lax.axis_index("x").reshape(1),
        ]
    )

    share = (col_norm[:, None] * features.astype(F32)).astype(BF16)
    own = lax.all_to_all(repeat(share, n_y), "y", 0, 0, tiled=True)
    other = lax.ppermute(own, "core", swap)

    blocks = pl.pallas_call(
        forward_kernel,
        out_shape=(jax.ShapeDtypeStruct((n_z, n, hidden), BF16),) * n_x,
        in_specs=[SMEM, VMEM, VMEM, VMEM],
        out_specs=(VMEM,) * n_x,
        scratch_shapes=[pltpu.VMEM((tile_rows, n, hidden), F32)],
        compiler_params=pltpu.CompilerParams(vmem_limit_bytes=40 * 2**20),
        name="forward_tiles",
    )(info, tiles, own, other)
    over_x = blocks[0].astype(F32)
    for d in range(1, n_x):
        over_x += lax.ppermute(blocks[d], "x", ring(n_x, d)).astype(F32)
    terms = lax.all_to_all(over_x.astype(BF16), "z", 0, 0, tiled=True)
    mixed = jnp.sum(terms.astype(F32), axis=0)

    high = mixed.astype(BF16)
    low = (mixed - high.astype(F32)).astype(BF16)
    rowsum = jnp.dot(high, weight, preferred_element_type=F32) + jnp.dot(
        low, weight, preferred_element_type=F32
    )
    pre = row_norm[:, None] * rowsum + bias[None, :]
    sigma = jax.nn.sigmoid(pre)
    output = (pre * sigma).astype(BF16)
    grad_pre = cotangent.astype(F32) * (sigma * (1.0 + pre * (1.0 - sigma)))
    grad_here = (grad_pre * row_norm[:, None]).astype(BF16)

    weight_part = lax.dot_general(
        high, grad_here, (((0,), (0,)), ((), ())), preferred_element_type=F32
    )
    bias_part = jnp.sum(grad_pre, axis=0)
    chunk = hidden // tile_cols
    both = jnp.concatenate(
        [
            (weight_part * scale).reshape(tile_cols, chunk, hidden),
            jnp.broadcast_to(bias_part * scale, (tile_cols, 8, hidden)),
        ],
        axis=1,
    ).astype(BF16)
    g0 = lax.all_to_all(repeat(grad_here, n_z), "z", 0, 0, tiled=True)
    g0, both = lax.optimization_barrier((g0, both))
    g = [g0]
    for d in range(1, n_x):
        g.append(lax.ppermute(g0, "x", [((i + d) % n_x, i) for i in range(n_x)]))
    both = jnp.sum(lax.all_to_all(both, ROW, 0, 0, tiled=True).astype(F32), axis=0)
    both = lax.all_to_all(repeat(both.astype(BF16), tile_rows), COL, 0, 0, tiled=True)
    both = jnp.sum(both.astype(F32), axis=0)
    grad_bias = both[chunk]
    chunk_here = both[:chunk].astype(BF16)
    chunk_other = lax.ppermute(chunk_here, "core", swap)
    first = lax.axis_index("core") == 0
    chunks = jnp.concatenate(
        [
            jnp.where(first, chunk_here, chunk_other),
            jnp.where(first, chunk_other, chunk_here),
        ],
        axis=0,
    )

    keep, send = pl.pallas_call(
        backward_kernel,
        out_shape=(
            jax.ShapeDtypeStruct((n_y, n, hidden), F32),
            jax.ShapeDtypeStruct((n_y, n, hidden), BF16),
        ),
        in_specs=[SMEM, VMEM, VMEM, VMEM, VMEM, VMEM],
        out_specs=(VMEM, VMEM),
        scratch_shapes=[pltpu.VMEM((tile_cols, n, hidden), F32)],
        compiler_params=pltpu.CompilerParams(vmem_limit_bytes=40 * 2**20),
        name="backward_tiles",
    )(info, tiles, *g)
    pair = (keep + lax.ppermute(send, "core", swap).astype(F32)).astype(BF16)
    last = jnp.concatenate([pair, repeat(chunks, n_y)], axis=1)
    last = lax.all_to_all(last, "y", 0, 0, tiled=True)
    column_total = jnp.sum(last[:, :n].astype(F32), axis=0)
    grad_weight = last[:, n:].reshape(hidden, hidden).astype(F32)
    grad_mixed = (col_norm[:, None] * column_total).astype(BF16)
    grad_features = lax.dot_general(
        grad_mixed, weight, (((1,), (1,)), ((), ())), preferred_element_type=F32
    ).astype(BF16)
    return (output, grad_features, grad_weight, grad_bias)


def solution(mesh):
    devices = mesh.devices
    sub = Mesh(devices.reshape(8, 2, 8, 4), ("y", "core", "z", "x"))
    by_col = ("z", "x", "y", "core")
    by_row = ("y", "core", "z", "x")
    in_specs = (
        P(by_col, None),
        P(by_col),
        P(),
        P(),
        P(ROW, COL, None, None),
        P(ROW, COL),
        P(ROW, COL, None, None, None),
        P(by_row),
        P(by_row, None),
    )
    out_specs = (P(by_row, None), P(by_col, None), P(), P())
    return jax.shard_map(body, mesh=sub, in_specs=in_specs, out_specs=out_specs, check_vma=False)
```

```python
import jax
import jax.numpy as jnp
from jax import lax
from jax.experimental import pallas as pl
from jax.experimental.pallas import tpu as pltpu
from jax.sharding import Mesh, PartitionSpec as P

COL = ("z", "x")
ROW = ("y", "core")
VMEM = pl.BlockSpec(memory_space=pltpu.VMEM)
SMEM = pl.BlockSpec(memory_space=pltpu.SMEM)
F32 = jnp.float32
BF16 = jnp.bfloat16


UNROLL = 4


def forward_kernel(info, tiles, own, other, out, total):
    slots = tiles.shape[0]
    count = info[2 * slots]
    core = info[2 * slots + 1]
    n_x, n_z = out.shape[:2]
    total[...] = jnp.zeros_like(total)

    def step(b, _):
        places, products = [], []
        for u in range(UNROLL):
            k = b * UNROLL + u
            r = info[k]
            c = info[slots + k]
            half = c // 2
            picked = jnp.where((c % 2) == core, own[half], other[half])
            product = jnp.dot(tiles[k], picked, preferred_element_type=F32)
            products.append(jnp.where(k < count, product, 0.0))
            places.append(r % n_x * n_z + r // n_x)
        for place, product in zip(places, products):
            total[place] += product
        return 0

    lax.fori_loop(0, (count + UNROLL - 1) // UNROLL, step, 0)
    out[...] = total[...].reshape(out.shape).astype(out.dtype)


def backward_kernel(info, tiles, g0, g1, g2, g3, keep, send, total):
    slots = tiles.shape[0]
    count = info[2 * slots]
    core = info[2 * slots + 1]
    here = info[2 * slots + 2]
    n_half = keep.shape[0]
    total[...] = jnp.zeros_like(total)

    def step(b, _):
        places, products = [], []
        for u in range(UNROLL):
            k = b * UNROLL + u
            r = info[k]
            c = info[slots + k]
            z = r // 4
            d = (r % 4 - here + 4) % 4
            picked = jnp.where(
                d < 2,
                jnp.where(d == 0, g0[z], g1[z]),
                jnp.where(d == 2, g2[z], g3[z]),
            )
            product = lax.dot_general(
                tiles[k], picked, (((0,), (0,)), ((), ())), preferred_element_type=F32
            )
            products.append(jnp.where(k < count, product, 0.0))
            places.append(jnp.where((c % 2) == core, 0, n_half) + c // 2)
        for place, product in zip(places, products):
            total[place] += product
        return 0

    lax.fori_loop(0, (count + UNROLL - 1) // UNROLL, step, 0)
    keep[...] = total[:n_half]
    send[...] = total[n_half:].astype(send.dtype)


def ring(n, d):
    return [(i, (i + d) % n) for i in range(n)]


def repeat(a, n):
    return jnp.broadcast_to(a[None], (n,) + a.shape)


def body(
    features, col_norm, weight, bias, tile_coords, tile_count, tile_values, row_norm, cotangent
):
    n, hidden = features.shape
    n_y, n_core = lax.axis_size("y"), lax.axis_size("core")
    n_z, n_x = lax.axis_size("z"), lax.axis_size("x")
    tile_rows, tile_cols = n_z * n_x, n_y * n_core
    scale = float(n * tile_rows * tile_cols) ** (-0.5)
    tiles = tile_values[0, 0]
    coords = tile_coords[0, 0]
    swap = [(0, 1), (1, 0)]
    info = jnp.concatenate(
        [
            coords[:, 0],
            coords[:, 1],
            tile_count[0],
            lax.axis_index("core").reshape(1),
            lax.axis_index("x").reshape(1),
        ]
    )

    share = (col_norm[:, None] * features.astype(F32)).astype(BF16)
    own = lax.all_to_all(repeat(share, n_y), "y", 0, 0, tiled=True)
    other = lax.ppermute(own, "core", swap)

    blocks = pl.pallas_call(
        forward_kernel,
        out_shape=jax.ShapeDtypeStruct((n_x, n_z, n, hidden), BF16),
        in_specs=[SMEM, VMEM, VMEM, VMEM],
        out_specs=VMEM,
        scratch_shapes=[pltpu.VMEM((tile_rows, n, hidden), F32)],
        compiler_params=pltpu.CompilerParams(vmem_limit_bytes=40 * 2**20),
        name="forward_tiles",
    )(info, tiles, own, other)
    over_x = jnp.sum(lax.all_to_all(blocks, "x", 0, 0, tiled=True).astype(F32), axis=0)
    terms = lax.all_to_all(over_x.astype(BF16), "z", 0, 0, tiled=True)
    mixed = jnp.sum(terms.astype(F32), axis=0)

    high = mixed.astype(BF16)
    low = (mixed - high.astype(F32)).astype(BF16)
    rowsum = jnp.dot(high, weight, preferred_element_type=F32) + jnp.dot(
        low, weight, preferred_element_type=F32
    )
    pre = row_norm[:, None] * rowsum + bias[None, :]
    sigma = jax.nn.sigmoid(pre)
    output = (pre * sigma).astype(BF16)
    grad_pre = cotangent.astype(F32) * (sigma * (1.0 + pre * (1.0 - sigma)))
    grad_here = (grad_pre * row_norm[:, None]).astype(BF16)

    weight_part = lax.dot_general(
        high, grad_here, (((0,), (0,)), ((), ())), preferred_element_type=F32
    )
    bias_part = jnp.sum(grad_pre, axis=0)
    chunk = hidden // tile_cols
    both = jnp.concatenate(
        [
            (weight_part * scale).reshape(tile_cols, chunk, hidden),
            jnp.broadcast_to(bias_part * scale, (tile_cols, 8, hidden)),
        ],
        axis=1,
    ).astype(BF16)
    g0 = lax.all_to_all(repeat(grad_here, n_z), "z", 0, 0, tiled=True)
    g0, both = lax.optimization_barrier((g0, both))
    g = [g0] + [lax.ppermute(g0, "x", ring(n_x, n_x - d)) for d in range(1, n_x)]
    both = jnp.sum(lax.all_to_all(both, ROW, 0, 0, tiled=True).astype(F32), axis=0)
    both = lax.all_to_all(repeat(both.astype(BF16), tile_rows), COL, 0, 0, tiled=True)
    both = jnp.sum(both.astype(F32), axis=0)
    grad_bias = both[chunk]
    chunk_here = both[:chunk].astype(BF16)
    chunk_other = lax.ppermute(chunk_here, "core", swap)
    first = lax.axis_index("core") == 0
    chunks = jnp.concatenate(
        [
            jnp.where(first, chunk_here, chunk_other),
            jnp.where(first, chunk_other, chunk_here),
        ],
        axis=0,
    )

    keep, send = pl.pallas_call(
        backward_kernel,
        out_shape=(
            jax.ShapeDtypeStruct((n_y, n, hidden), F32),
            jax.ShapeDtypeStruct((n_y, n, hidden), BF16),
        ),
        in_specs=[SMEM, VMEM, VMEM, VMEM, VMEM, VMEM],
        out_specs=(VMEM, VMEM),
        scratch_shapes=[pltpu.VMEM((tile_cols, n, hidden), F32)],
        compiler_params=pltpu.CompilerParams(vmem_limit_bytes=40 * 2**20),
        name="backward_tiles",
    )(info, tiles, *g)
    pair = (keep + lax.ppermute(send, "core", swap).astype(F32)).astype(BF16)
    last = jnp.concatenate([pair, repeat(chunks, n_y)], axis=1)
    last = lax.all_to_all(last, "y", 0, 0, tiled=True)
    column_total = jnp.sum(last[:, :n].astype(F32), axis=0)
    grad_weight = last[:, n:].reshape(hidden, hidden).astype(F32)
    grad_mixed = (col_norm[:, None] * column_total).astype(BF16)
    grad_features = lax.dot_general(
        grad_mixed, weight, (((1,), (1,)), ((), ())), preferred_element_type=F32
    ).astype(BF16)
    return (output, grad_features, grad_weight, grad_bias)


def solution(mesh):
    devices = mesh.devices
    sub = Mesh(devices.reshape(8, 2, 8, 4), ("y", "core", "z", "x"))
    by_col = ("z", "x", "y", "core")
    by_row = ("y", "core", "z", "x")
    in_specs = (
        P(by_col, None),
        P(by_col),
        P(),
        P(),
        P(ROW, COL, None, None),
        P(ROW, COL),
        P(ROW, COL, None, None, None),
        P(by_row),
        P(by_row, None),
    )
    out_specs = (P(by_row, None), P(by_col, None), P(), P())
    return jax.shard_map(body, mesh=sub, in_specs=in_specs, out_specs=out_specs, check_vma=False)
```

```python
import jax
import jax.numpy as jnp
from jax import lax
from jax.experimental import pallas as pl
from jax.experimental.pallas import tpu as pltpu
from jax.sharding import Mesh, PartitionSpec as P

COL = ("z", "x")
ROW = ("y", "core")
VMEM = pl.BlockSpec(memory_space=pltpu.VMEM)
SMEM = pl.BlockSpec(memory_space=pltpu.SMEM)
F32 = jnp.float32
BF16 = jnp.bfloat16


UNROLL = 4


def forward_kernel(info, tiles, own, other, out, total):
    slots = tiles.shape[0]
    count = info[2 * slots]
    core = info[2 * slots + 1]
    n_x, n_z = out.shape[:2]
    total[...] = jnp.zeros_like(total)

    def step(b, _):
        places, products = [], []
        for u in range(UNROLL):
            k = b * UNROLL + u
            r = info[k]
            c = info[slots + k]
            half = c // 2
            picked = jnp.where((c % 2) == core, own[half], other[half])
            product = jnp.dot(tiles[k], picked, preferred_element_type=F32)
            products.append(jnp.where(k < count, product, 0.0))
            places.append(r % n_x * n_z + r // n_x)
        for place, product in zip(places, products):
            total[place] += product
        return 0

    lax.fori_loop(0, (count + UNROLL - 1) // UNROLL, step, 0)
    out[...] = total[...].reshape(out.shape).astype(out.dtype)


def backward_kernel(info, tiles, g, keep, send, total):
    slots = tiles.shape[0]
    count = info[2 * slots]
    core = info[2 * slots + 1]
    n_x, n_z = 4, g.shape[0] // 4
    n_half = keep.shape[0]
    total[...] = jnp.zeros_like(total)

    def step(b, _):
        places, products = [], []
        for u in range(UNROLL):
            k = b * UNROLL + u
            r = info[k]
            c = info[slots + k]
            picked = g[r % n_x * n_z + r // n_x]
            product = lax.dot_general(
                tiles[k], picked, (((0,), (0,)), ((), ())), preferred_element_type=F32
            )
            products.append(jnp.where(k < count, product, 0.0))
            places.append(jnp.where((c % 2) == core, 0, n_half) + c // 2)
        for place, product in zip(places, products):
            total[place] += product
        return 0

    lax.fori_loop(0, (count + UNROLL - 1) // UNROLL, step, 0)
    keep[...] = total[:n_half]
    send[...] = total[n_half:].astype(send.dtype)


def repeat(a, n):
    return jnp.broadcast_to(a[None], (n,) + a.shape)


def body(
    features, col_norm, weight, bias, tile_coords, tile_count, tile_values, row_norm, cotangent
):
    n, hidden = features.shape
    n_y, n_core = lax.axis_size("y"), lax.axis_size("core")
    n_z, n_x = lax.axis_size("z"), lax.axis_size("x")
    tile_rows, tile_cols = n_z * n_x, n_y * n_core
    scale = float(n * tile_rows * tile_cols) ** (-0.5)
    tiles = tile_values[0, 0]
    coords = tile_coords[0, 0]
    swap = [(0, 1), (1, 0)]
    info = jnp.concatenate(
        [
            coords[:, 0],
            coords[:, 1],
            tile_count[0],
            lax.axis_index("core").reshape(1),
        ]
    )

    share = (col_norm[:, None] * features.astype(F32)).astype(BF16)
    own = lax.all_to_all(repeat(share, n_y), "y", 0, 0, tiled=True)
    other = lax.ppermute(own, "core", swap)

    blocks = pl.pallas_call(
        forward_kernel,
        out_shape=jax.ShapeDtypeStruct((n_x, n_z, n, hidden), BF16),
        in_specs=[SMEM, VMEM, VMEM, VMEM],
        out_specs=VMEM,
        scratch_shapes=[pltpu.VMEM((tile_rows, n, hidden), F32)],
        compiler_params=pltpu.CompilerParams(vmem_limit_bytes=40 * 2**20),
        name="forward_tiles",
    )(info, tiles, own, other)
    over_x = jnp.sum(lax.all_to_all(blocks, "x", 0, 0, tiled=True).astype(F32), axis=0)
    terms = lax.all_to_all(over_x.astype(BF16), "z", 0, 0, tiled=True)
    mixed = jnp.sum(terms.astype(F32), axis=0)

    high = mixed.astype(BF16)
    low = (mixed - high.astype(F32)).astype(BF16)
    rowsum = jnp.dot(high, weight, preferred_element_type=F32) + jnp.dot(
        low, weight, preferred_element_type=F32
    )
    pre = row_norm[:, None] * rowsum + bias[None, :]
    sigma = jax.nn.sigmoid(pre)
    output = (pre * sigma).astype(BF16)
    grad_pre = cotangent.astype(F32) * (sigma * (1.0 + pre * (1.0 - sigma)))
    grad_here = (grad_pre * row_norm[:, None]).astype(BF16)

    weight_part = lax.dot_general(
        high, grad_here, (((0,), (0,)), ((), ())), preferred_element_type=F32
    )
    bias_part = jnp.sum(grad_pre, axis=0)
    chunk = hidden // tile_cols
    both = jnp.concatenate(
        [
            (weight_part * scale).reshape(tile_cols, chunk, hidden),
            jnp.broadcast_to(bias_part * scale, (tile_cols, 8, hidden)),
        ],
        axis=1,
    ).astype(BF16)
    g0 = lax.all_to_all(repeat(grad_here, n_z), "z", 0, 0, tiled=True)
    g0, both = lax.optimization_barrier((g0, both))
    g = lax.all_gather(g0, "x", axis=0, tiled=True)
    both = jnp.sum(lax.all_to_all(both, ROW, 0, 0, tiled=True).astype(F32), axis=0)
    both = lax.all_to_all(repeat(both.astype(BF16), tile_rows), COL, 0, 0, tiled=True)
    both = jnp.sum(both.astype(F32), axis=0)
    grad_bias = both[chunk]
    chunk_here = both[:chunk].astype(BF16)
    chunk_other = lax.ppermute(chunk_here, "core", swap)
    first = lax.axis_index("core") == 0
    chunks = jnp.concatenate(
        [
            jnp.where(first, chunk_here, chunk_other),
            jnp.where(first, chunk_other, chunk_here),
        ],
        axis=0,
    )

    keep, send = pl.pallas_call(
        backward_kernel,
        out_shape=(
            jax.ShapeDtypeStruct((n_y, n, hidden), F32),
            jax.ShapeDtypeStruct((n_y, n, hidden), BF16),
        ),
        in_specs=[SMEM, VMEM, VMEM],
        out_specs=(VMEM, VMEM),
        scratch_shapes=[pltpu.VMEM((tile_cols, n, hidden), F32)],
        compiler_params=pltpu.CompilerParams(vmem_limit_bytes=40 * 2**20),
        name="backward_tiles",
    )(info, tiles, g)
    pair = (keep + lax.ppermute(send, "core", swap).astype(F32)).astype(BF16)
    last = jnp.concatenate([pair, repeat(chunks, n_y)], axis=1)
    last = lax.all_to_all(last, "y", 0, 0, tiled=True)
    column_total = jnp.sum(last[:, :n].astype(F32), axis=0)
    grad_weight = last[:, n:].reshape(hidden, hidden).astype(F32)
    grad_mixed = (col_norm[:, None] * column_total).astype(BF16)
    grad_features = lax.dot_general(
        grad_mixed, weight, (((1,), (1,)), ((), ())), preferred_element_type=F32
    ).astype(BF16)
    return (output, grad_features, grad_weight, grad_bias)


def solution(mesh):
    devices = mesh.devices
    sub = Mesh(devices.reshape(8, 2, 8, 4), ("y", "core", "z", "x"))
    by_col = ("z", "x", "y", "core")
    by_row = ("y", "core", "z", "x")
    in_specs = (
        P(by_col, None),
        P(by_col),
        P(),
        P(),
        P(ROW, COL, None, None),
        P(ROW, COL),
        P(ROW, COL, None, None, None),
        P(by_row),
        P(by_row, None),
    )
    out_specs = (P(by_row, None), P(by_col, None), P(), P())
    return jax.shard_map(body, mesh=sub, in_specs=in_specs, out_specs=out_specs, check_vma=False)
```

```python
import jax
import jax.numpy as jnp
from jax import lax
from jax.experimental import pallas as pl
from jax.experimental.pallas import tpu as pltpu
from jax.sharding import Mesh, PartitionSpec as P

COL = ("z", "x")
ROW = ("y", "core")
VMEM = pl.BlockSpec(memory_space=pltpu.VMEM)
SMEM = pl.BlockSpec(memory_space=pltpu.SMEM)
F32 = jnp.float32
BF16 = jnp.bfloat16


UNROLL = 4


def forward_kernel(info, tiles, own, other, out, total):
    slots = tiles.shape[0]
    count = info[2 * slots]
    core = info[2 * slots + 1]
    n_x, n_z = out.shape[:2]
    total[...] = jnp.zeros_like(total)

    def step(b, _):
        places, products = [], []
        for u in range(UNROLL):
            k = b * UNROLL + u
            r = info[k]
            c = info[slots + k]
            half = c // 2
            picked = jnp.where((c % 2) == core, own[half], other[half])
            product = jnp.dot(tiles[k], picked, preferred_element_type=F32)
            products.append(jnp.where(k < count, product, 0.0))
            places.append(r % n_x * n_z + r // n_x)
        for place, product in zip(places, products):
            total[place] += product
        return 0

    lax.fori_loop(0, (count + UNROLL - 1) // UNROLL, step, 0)
    out[...] = total[...].reshape(out.shape).astype(out.dtype)


def backward_kernel(info, tiles, g0, g1, g2_low, g2_high, g3, keep, send, total):
    slots = tiles.shape[0]
    count = info[2 * slots]
    core = info[2 * slots + 1]
    here = info[2 * slots + 2]
    n_half = keep.shape[0]
    half_z = g2_low.shape[0]
    total[...] = jnp.zeros_like(total)

    def step(b, _):
        places, products = [], []
        for u in range(UNROLL):
            k = b * UNROLL + u
            r = info[k]
            c = info[slots + k]
            z = r // 4
            d = (r % 4 - here + 4) % 4
            far = jnp.where(z < half_z, g2_low[z % half_z], g2_high[z % half_z])
            picked = jnp.where(
                d < 2,
                jnp.where(d == 0, g0[z], g1[z]),
                jnp.where(d == 2, far, g3[z]),
            )
            product = lax.dot_general(
                tiles[k], picked, (((0,), (0,)), ((), ())), preferred_element_type=F32
            )
            products.append(jnp.where(k < count, product, 0.0))
            places.append(jnp.where((c % 2) == core, 0, n_half) + c // 2)
        for place, product in zip(places, products):
            total[place] += product
        return 0

    lax.fori_loop(0, (count + UNROLL - 1) // UNROLL, step, 0)
    keep[...] = total[:n_half]
    send[...] = total[n_half:].astype(send.dtype)


def ring(n, d):
    return [(i, (i + d) % n) for i in range(n)]


def repeat(a, n):
    return jnp.broadcast_to(a[None], (n,) + a.shape)


def body(
    features, col_norm, weight, bias, tile_coords, tile_count, tile_values, row_norm, cotangent
):
    n, hidden = features.shape
    n_y, n_core = lax.axis_size("y"), lax.axis_size("core")
    n_z, n_x = lax.axis_size("z"), lax.axis_size("x")
    tile_rows, tile_cols = n_z * n_x, n_y * n_core
    scale = float(n * tile_rows * tile_cols) ** (-0.5)
    tiles = tile_values[0, 0]
    coords = tile_coords[0, 0]
    swap = [(0, 1), (1, 0)]
    info = jnp.concatenate(
        [
            coords[:, 0],
            coords[:, 1],
            tile_count[0],
            lax.axis_index("core").reshape(1),
            lax.axis_index("x").reshape(1),
        ]
    )

    share = (col_norm[:, None] * features.astype(F32)).astype(BF16)
    own = lax.all_to_all(repeat(share, n_y), "y", 0, 0, tiled=True)
    other = lax.ppermute(own, "core", swap)

    blocks = pl.pallas_call(
        forward_kernel,
        out_shape=jax.ShapeDtypeStruct((n_x, n_z, n, hidden), BF16),
        in_specs=[SMEM, VMEM, VMEM, VMEM],
        out_specs=VMEM,
        scratch_shapes=[pltpu.VMEM((tile_rows, n, hidden), F32)],
        compiler_params=pltpu.CompilerParams(vmem_limit_bytes=40 * 2**20),
        name="forward_tiles",
    )(info, tiles, own, other)
    over_x = jnp.sum(lax.all_to_all(blocks, "x", 0, 0, tiled=True).astype(F32), axis=0)
    terms = lax.all_to_all(over_x.astype(BF16), "z", 0, 0, tiled=True)
    mixed = jnp.sum(terms.astype(F32), axis=0)

    high = mixed.astype(BF16)
    low = (mixed - high.astype(F32)).astype(BF16)
    rowsum = jnp.dot(high, weight, preferred_element_type=F32) + jnp.dot(
        low, weight, preferred_element_type=F32
    )
    pre = row_norm[:, None] * rowsum + bias[None, :]
    sigma = jax.nn.sigmoid(pre)
    output = (pre * sigma).astype(BF16)
    grad_pre = cotangent.astype(F32) * (sigma * (1.0 + pre * (1.0 - sigma)))
    grad_here = (grad_pre * row_norm[:, None]).astype(BF16)

    weight_part = lax.dot_general(
        high, grad_here, (((0,), (0,)), ((), ())), preferred_element_type=F32
    )
    bias_part = jnp.sum(grad_pre, axis=0)
    chunk = hidden // tile_cols
    both = jnp.concatenate(
        [
            (weight_part * scale).reshape(tile_cols, chunk, hidden),
            jnp.broadcast_to(bias_part * scale, (tile_cols, 8, hidden)),
        ],
        axis=1,
    ).astype(BF16)
    g0 = lax.all_to_all(repeat(grad_here, n_z), "z", 0, 0, tiled=True)
    g0, both = lax.optimization_barrier((g0, both))
    g1 = lax.ppermute(g0, "x", ring(n_x, n_x - 1))
    g3 = lax.ppermute(g0, "x", ring(n_x, 1))
    g2_low = lax.ppermute(g1[: n_z // 2], "x", ring(n_x, n_x - 1))
    g2_high = lax.ppermute(g3[n_z // 2 :], "x", ring(n_x, 1))
    g = [g0, g1, g2_low, g2_high, g3]
    both = jnp.sum(lax.all_to_all(both, ROW, 0, 0, tiled=True).astype(F32), axis=0)
    both = lax.all_to_all(repeat(both.astype(BF16), tile_rows), COL, 0, 0, tiled=True)
    both = jnp.sum(both.astype(F32), axis=0)
    grad_bias = both[chunk]
    chunk_here = both[:chunk].astype(BF16)
    chunk_other = lax.ppermute(chunk_here, "core", swap)
    first = lax.axis_index("core") == 0
    chunks = jnp.concatenate(
        [
            jnp.where(first, chunk_here, chunk_other),
            jnp.where(first, chunk_other, chunk_here),
        ],
        axis=0,
    )

    keep, send = pl.pallas_call(
        backward_kernel,
        out_shape=(
            jax.ShapeDtypeStruct((n_y, n, hidden), F32),
            jax.ShapeDtypeStruct((n_y, n, hidden), BF16),
        ),
        in_specs=[SMEM] + [VMEM] * 6,
        out_specs=(VMEM, VMEM),
        scratch_shapes=[pltpu.VMEM((tile_cols, n, hidden), F32)],
        compiler_params=pltpu.CompilerParams(vmem_limit_bytes=40 * 2**20),
        name="backward_tiles",
    )(info, tiles, *g)
    pair = (keep + lax.ppermute(send, "core", swap).astype(F32)).astype(BF16)
    last = jnp.concatenate([pair, repeat(chunks, n_y)], axis=1)
    last = lax.all_to_all(last, "y", 0, 0, tiled=True)
    column_total = jnp.sum(last[:, :n].astype(F32), axis=0)
    grad_weight = last[:, n:].reshape(hidden, hidden).astype(F32)
    grad_mixed = (col_norm[:, None] * column_total).astype(BF16)
    grad_features = lax.dot_general(
        grad_mixed, weight, (((1,), (1,)), ((), ())), preferred_element_type=F32
    ).astype(BF16)
    return (output, grad_features, grad_weight, grad_bias)


def solution(mesh):
    devices = mesh.devices
    sub = Mesh(devices.reshape(8, 2, 8, 4), ("y", "core", "z", "x"))
    by_col = ("z", "x", "y", "core")
    by_row = ("y", "core", "z", "x")
    in_specs = (
        P(by_col, None),
        P(by_col),
        P(),
        P(),
        P(ROW, COL, None, None),
        P(ROW, COL),
        P(ROW, COL, None, None, None),
        P(by_row),
        P(by_row, None),
    )
    out_specs = (P(by_row, None), P(by_col, None), P(), P())
    return jax.shard_map(body, mesh=sub, in_specs=in_specs, out_specs=out_specs, check_vma=False)
```

```python
import jax
import jax.numpy as jnp
from jax import lax
from jax.experimental import pallas as pl
from jax.experimental.pallas import tpu as pltpu
from jax.sharding import Mesh, PartitionSpec as P

COL = ("z", "x")
ROW = ("y", "core")
VMEM = pl.BlockSpec(memory_space=pltpu.VMEM)
SMEM = pl.BlockSpec(memory_space=pltpu.SMEM)
F32 = jnp.float32
BF16 = jnp.bfloat16


UNROLL = 4


def forward_kernel(info, tiles, own, other, out, total):
    slots = tiles.shape[0]
    count = info[2 * slots]
    core = info[2 * slots + 1]
    n_x, n_z = out.shape[:2]
    total[...] = jnp.zeros_like(total)

    def step(b, _):
        places, products = [], []
        for u in range(UNROLL):
            k = b * UNROLL + u
            r = info[k]
            c = info[slots + k]
            half = c // 2
            picked = jnp.where((c % 2) == core, own[half], other[half])
            product = jnp.dot(tiles[k], picked, preferred_element_type=F32)
            products.append(jnp.where(k < count, product, 0.0))
            places.append(r % n_x * n_z + r // n_x)
        for place, product in zip(places, products):
            total[place] += product
        return 0

    lax.fori_loop(0, (count + UNROLL - 1) // UNROLL, step, 0)
    out[...] = total[...].reshape(out.shape).astype(out.dtype)


def backward_kernel(info, tiles, g0, g1, g2_low, g2_high, g3, keep, send, total):
    slots = tiles.shape[0]
    count = info[2 * slots]
    core = info[2 * slots + 1]
    here = info[2 * slots + 2]
    n_half = keep.shape[0]
    half_z = g2_low.shape[0]
    total[...] = jnp.zeros_like(total)

    def step(b, _):
        places, products = [], []
        for u in range(UNROLL):
            k = b * UNROLL + u
            r = info[k]
            c = info[slots + k]
            z = r // 4
            d = (r % 4 - here + 4) % 4
            far = jnp.where(z < half_z, g2_low[z % half_z], g2_high[z % half_z])
            picked = jnp.where(
                d < 2,
                jnp.where(d == 0, g0[z], g1[z]),
                jnp.where(d == 2, far, g3[z]),
            )
            product = lax.dot_general(
                tiles[k], picked, (((0,), (0,)), ((), ())), preferred_element_type=F32
            )
            products.append(jnp.where(k < count, product, 0.0))
            places.append(jnp.where((c % 2) == core, 0, n_half) + c // 2)
        for place, product in zip(places, products):
            total[place] += product
        return 0

    lax.fori_loop(0, (count + UNROLL - 1) // UNROLL, step, 0)
    keep[...] = total[:n_half]
    send[...] = total[n_half:].astype(send.dtype)


def ring(n, d):
    return [(i, (i + d) % n) for i in range(n)]


def repeat(a, n):
    return jnp.broadcast_to(a[None], (n,) + a.shape)


def body(
    features, col_norm, weight, bias, tile_coords, tile_count, tile_values, row_norm, cotangent
):
    n, hidden = features.shape
    n_y, n_core = lax.axis_size("y"), lax.axis_size("core")
    n_z, n_x = lax.axis_size("z"), lax.axis_size("x")
    tile_rows, tile_cols = n_z * n_x, n_y * n_core
    scale = float(n * tile_rows * tile_cols) ** (-0.5)
    tiles = tile_values[0, 0]
    coords = tile_coords[0, 0]
    swap = [(0, 1), (1, 0)]
    info = jnp.concatenate(
        [
            coords[:, 0],
            coords[:, 1],
            tile_count[0],
            lax.axis_index("core").reshape(1),
            lax.axis_index("x").reshape(1),
        ]
    )

    share = (col_norm[:, None] * features.astype(F32)).astype(BF16)
    own = lax.all_to_all(repeat(share, n_y), "y", 0, 0, tiled=True)
    other = lax.ppermute(own, "core", swap)

    blocks = pl.pallas_call(
        forward_kernel,
        out_shape=jax.ShapeDtypeStruct((n_x, n_z, n, hidden), BF16),
        in_specs=[SMEM, VMEM, VMEM, VMEM],
        out_specs=VMEM,
        scratch_shapes=[pltpu.VMEM((tile_rows, n, hidden), F32)],
        compiler_params=pltpu.CompilerParams(vmem_limit_bytes=40 * 2**20),
        name="forward_tiles",
    )(info, tiles, own, other)
    over_x = jnp.sum(lax.all_to_all(blocks, "x", 0, 0, tiled=True).astype(F32), axis=0)
    terms = lax.all_to_all(over_x.astype(BF16), "z", 0, 0, tiled=True)
    mixed = jnp.sum(terms.astype(F32), axis=0)

    high = mixed.astype(BF16)
    low = (mixed - high.astype(F32)).astype(BF16)
    rowsum = jnp.dot(high, weight, preferred_element_type=F32) + jnp.dot(
        low, weight, preferred_element_type=F32
    )
    pre = row_norm[:, None] * rowsum + bias[None, :]
    sigma = jax.nn.sigmoid(pre)
    output = (pre * sigma).astype(BF16)
    grad_pre = cotangent.astype(F32) * (sigma * (1.0 + pre * (1.0 - sigma)))
    grad_here = (grad_pre * row_norm[:, None]).astype(BF16)

    weight_part = lax.dot_general(
        high, grad_here, (((0,), (0,)), ((), ())), preferred_element_type=F32
    )
    bias_part = jnp.sum(grad_pre, axis=0)
    chunk = hidden // tile_cols
    both = jnp.concatenate(
        [
            (weight_part * scale).reshape(tile_cols, chunk, hidden),
            jnp.broadcast_to(bias_part * scale, (tile_cols, 8, hidden)),
        ],
        axis=1,
    ).astype(BF16)
    g0 = lax.all_to_all(repeat(grad_here, n_z), "z", 0, 0, tiled=True)
    g0, both = lax.optimization_barrier((g0, both))
    g1 = lax.ppermute(g0, "x", ring(n_x, n_x - 1))
    g3 = lax.ppermute(g0, "x", ring(n_x, 1))
    g2_low = lax.ppermute(g1[: n_z // 2], "x", ring(n_x, n_x - 1))
    g2_high = lax.ppermute(g3[n_z // 2 :], "x", ring(n_x, 1))
    g = [g0, g1, g2_low, g2_high, g3]
    both = jnp.sum(lax.all_to_all(both, ROW, 0, 0, tiled=True).astype(F32), axis=0)
    both = lax.all_to_all(repeat(both.astype(BF16), tile_rows), COL, 0, 0, tiled=True)
    both = jnp.sum(both.astype(F32), axis=0)
    grad_bias = both[chunk]
    chunk_here = both[:chunk].astype(BF16)

    keep, send = pl.pallas_call(
        backward_kernel,
        out_shape=(
            jax.ShapeDtypeStruct((n_y, n, hidden), F32),
            jax.ShapeDtypeStruct((n_y, n, hidden), BF16),
        ),
        in_specs=[SMEM] + [VMEM] * 6,
        out_specs=(VMEM, VMEM),
        scratch_shapes=[pltpu.VMEM((tile_cols, n, hidden), F32)],
        compiler_params=pltpu.CompilerParams(vmem_limit_bytes=40 * 2**20),
        name="backward_tiles",
    )(info, tiles, *g)
    pair = (keep + lax.ppermute(send, "core", swap).astype(F32)).astype(BF16)
    last = jnp.concatenate([pair, repeat(chunk_here, n_y)], axis=1)
    last = lax.all_to_all(last, "y", 0, 0, tiled=True)
    column_total = jnp.sum(last[:, :n].astype(F32), axis=0)
    chunks = last[:, n:]
    chunks_other = lax.ppermute(chunks, "core", swap)
    first = lax.axis_index("core") == 0
    grad_weight = jnp.concatenate(
        [jnp.where(first, chunks, chunks_other), jnp.where(first, chunks_other, chunks)], axis=1
    )
    grad_weight = grad_weight.reshape(hidden, hidden).astype(F32)
    grad_mixed = (col_norm[:, None] * column_total).astype(BF16)
    grad_features = lax.dot_general(
        grad_mixed, weight, (((1,), (1,)), ((), ())), preferred_element_type=F32
    ).astype(BF16)
    return (output, grad_features, grad_weight, grad_bias)


def solution(mesh):
    devices = mesh.devices
    sub = Mesh(devices.reshape(8, 2, 8, 4), ("y", "core", "z", "x"))
    by_col = ("z", "x", "y", "core")
    by_row = ("y", "core", "z", "x")
    in_specs = (
        P(by_col, None),
        P(by_col),
        P(),
        P(),
        P(ROW, COL, None, None),
        P(ROW, COL),
        P(ROW, COL, None, None, None),
        P(by_row),
        P(by_row, None),
    )
    out_specs = (P(by_row, None), P(by_col, None), P(), P())
    return jax.shard_map(body, mesh=sub, in_specs=in_specs, out_specs=out_specs, check_vma=False)
```

```python
import jax
import jax.numpy as jnp
from jax import lax
from jax.experimental import pallas as pl
from jax.experimental.pallas import tpu as pltpu
from jax.sharding import Mesh, PartitionSpec as P

COL = ("z", "x")
ROW = ("y", "core")
VMEM = pl.BlockSpec(memory_space=pltpu.VMEM)
SMEM = pl.BlockSpec(memory_space=pltpu.SMEM)
F32 = jnp.float32
BF16 = jnp.bfloat16


UNROLL = 4


def forward_kernel(info, tiles, own, other, out, total):
    slots = tiles.shape[0]
    count = info[2 * slots]
    core = info[2 * slots + 1]
    n_x, n_z = out.shape[:2]
    total[...] = jnp.zeros_like(total)

    def step(b, _):
        places, products = [], []
        for u in range(UNROLL):
            k = b * UNROLL + u
            r = info[k]
            c = info[slots + k]
            half = c // 2
            picked = jnp.where((c % 2) == core, own[half], other[half])
            product = jnp.dot(tiles[k], picked, preferred_element_type=F32)
            products.append(jnp.where(k < count, product, 0.0))
            places.append(r % n_x * n_z + r // n_x)
        for place, product in zip(places, products):
            total[place] += product
        return 0

    lax.fori_loop(0, (count + UNROLL - 1) // UNROLL, step, 0)
    out[...] = total[...].reshape(out.shape).astype(out.dtype)


def backward_kernel(info, tiles, g0, g1, g2_low, g2_high, g3, keep, send, total):
    slots = tiles.shape[0]
    count = info[2 * slots]
    core = info[2 * slots + 1]
    here = info[2 * slots + 2]
    n_half = keep.shape[0]
    half_z = g2_low.shape[0]
    total[...] = jnp.zeros_like(total)

    def step(b, _):
        places, products = [], []
        for u in range(UNROLL):
            k = b * UNROLL + u
            r = info[k]
            c = info[slots + k]
            z = r // 4
            d = (r % 4 - here + 4) % 4
            far = jnp.where(z < half_z, g2_low[z % half_z], g2_high[z % half_z])
            picked = jnp.where(
                d < 2,
                jnp.where(d == 0, g0[z], g1[z]),
                jnp.where(d == 2, far, g3[z]),
            )
            product = lax.dot_general(
                tiles[k], picked, (((0,), (0,)), ((), ())), preferred_element_type=F32
            )
            products.append(jnp.where(k < count, product, 0.0))
            places.append(jnp.where((c % 2) == core, 0, n_half) + c // 2)
        for place, product in zip(places, products):
            total[place] += product
        return 0

    lax.fori_loop(0, (count + UNROLL - 1) // UNROLL, step, 0)
    keep[...] = total[:n_half]
    send[...] = total[n_half:].astype(send.dtype)


def ring(n, d):
    return [(i, (i + d) % n) for i in range(n)]


def repeat(a, n):
    return jnp.broadcast_to(a[None], (n,) + a.shape)


def body(
    features, col_norm, weight, bias, tile_coords, tile_count, tile_values, row_norm, cotangent
):
    n, hidden = features.shape
    n_y, n_core = lax.axis_size("y"), lax.axis_size("core")
    n_z, n_x = lax.axis_size("z"), lax.axis_size("x")
    tile_rows, tile_cols = n_z * n_x, n_y * n_core
    scale = float(n * tile_rows * tile_cols) ** (-0.5)
    tiles = tile_values[0, 0]
    coords = tile_coords[0, 0]
    swap = [(0, 1), (1, 0)]
    info = jnp.concatenate(
        [
            coords[:, 0],
            coords[:, 1],
            tile_count[0],
            lax.axis_index("core").reshape(1),
            lax.axis_index("x").reshape(1),
        ]
    )

    share = (col_norm[:, None] * features.astype(F32)).astype(BF16)
    own = lax.all_to_all(repeat(share, n_y), "y", 0, 0, tiled=True)
    other = lax.ppermute(own, "core", swap)

    blocks = pl.pallas_call(
        forward_kernel,
        out_shape=jax.ShapeDtypeStruct((n_x, n_z, n, hidden), BF16),
        in_specs=[SMEM, VMEM, VMEM, VMEM],
        out_specs=VMEM,
        scratch_shapes=[pltpu.VMEM((tile_rows, n, hidden), F32)],
        compiler_params=pltpu.CompilerParams(vmem_limit_bytes=40 * 2**20),
        name="forward_tiles",
    )(info, tiles, own, other)
    over_x = jnp.sum(lax.all_to_all(blocks, "x", 0, 0, tiled=True).astype(F32), axis=0)
    terms = lax.all_to_all(over_x.astype(BF16), "z", 0, 0, tiled=True)
    mixed = jnp.sum(terms.astype(F32), axis=0)

    high = mixed.astype(BF16)
    low = (mixed - high.astype(F32)).astype(BF16)
    rowsum = jnp.dot(high, weight, preferred_element_type=F32) + jnp.dot(
        low, weight, preferred_element_type=F32
    )
    pre = row_norm[:, None] * rowsum + bias[None, :]
    sigma = jax.nn.sigmoid(pre)
    output = (pre * sigma).astype(BF16)
    grad_pre = cotangent.astype(F32) * (sigma * (1.0 + pre * (1.0 - sigma)))
    grad_here = (grad_pre * row_norm[:, None]).astype(BF16)

    weight_part = lax.dot_general(
        high, grad_here, (((0,), (0,)), ((), ())), preferred_element_type=F32
    )
    bias_part = jnp.sum(grad_pre, axis=0) * scale
    chunk = hidden // tile_cols
    first = lax.axis_index("core") == 0
    pairs = (weight_part * scale).reshape(n_y, n_core, chunk, hidden)
    away = jnp.concatenate(
        [
            jnp.where(first, pairs[:, 1], pairs[:, 0]),
            jnp.broadcast_to(bias_part, (1, chunk, hidden)),
        ],
        axis=0,
    ).astype(BF16)
    away = lax.ppermute(away, "core", swap).astype(F32)
    both = jnp.concatenate(
        [
            jnp.where(first, pairs[:, 0], pairs[:, 1]) + away[:n_y],
            jnp.broadcast_to(bias_part + away[n_y, 0], (n_y, 8, hidden)),
        ],
        axis=1,
    ).astype(BF16)
    g0 = lax.all_to_all(repeat(grad_here, n_z), "z", 0, 0, tiled=True)
    g0, both = lax.optimization_barrier((g0, both))
    g1 = lax.ppermute(g0, "x", ring(n_x, n_x - 1))
    g3 = lax.ppermute(g0, "x", ring(n_x, 1))
    g2_low = lax.ppermute(g1[: n_z // 2], "x", ring(n_x, n_x - 1))
    g2_high = lax.ppermute(g3[n_z // 2 :], "x", ring(n_x, 1))
    g = [g0, g1, g2_low, g2_high, g3]
    both = jnp.sum(lax.all_to_all(both, "y", 0, 0, tiled=True).astype(F32), axis=0)
    both = lax.all_to_all(repeat(both.astype(BF16), tile_rows), COL, 0, 0, tiled=True)
    both = jnp.sum(both.astype(F32), axis=0)
    grad_bias = both[chunk]
    chunk_here = both[:chunk].astype(BF16)

    keep, send = pl.pallas_call(
        backward_kernel,
        out_shape=(
            jax.ShapeDtypeStruct((n_y, n, hidden), F32),
            jax.ShapeDtypeStruct((n_y, n, hidden), BF16),
        ),
        in_specs=[SMEM] + [VMEM] * 6,
        out_specs=(VMEM, VMEM),
        scratch_shapes=[pltpu.VMEM((tile_cols, n, hidden), F32)],
        compiler_params=pltpu.CompilerParams(vmem_limit_bytes=40 * 2**20),
        name="backward_tiles",
    )(info, tiles, *g)
    pair = (keep + lax.ppermute(send, "core", swap).astype(F32)).astype(BF16)
    last = jnp.concatenate([pair, repeat(chunk_here, n_y)], axis=1)
    last = lax.all_to_all(last, "y", 0, 0, tiled=True)
    column_total = jnp.sum(last[:, :n].astype(F32), axis=0)
    chunks = last[:, n:]
    chunks_other = lax.ppermute(chunks, "core", swap)
    grad_weight = jnp.concatenate(
        [jnp.where(first, chunks, chunks_other), jnp.where(first, chunks_other, chunks)], axis=1
    )
    grad_weight = grad_weight.reshape(hidden, hidden).astype(F32)
    grad_mixed = (col_norm[:, None] * column_total).astype(BF16)
    grad_features = lax.dot_general(
        grad_mixed, weight, (((1,), (1,)), ((), ())), preferred_element_type=F32
    ).astype(BF16)
    return (output, grad_features, grad_weight, grad_bias)


def solution(mesh):
    devices = mesh.devices
    sub = Mesh(devices.reshape(8, 2, 8, 4), ("y", "core", "z", "x"))
    by_col = ("z", "x", "y", "core")
    by_row = ("y", "core", "z", "x")
    in_specs = (
        P(by_col, None),
        P(by_col),
        P(),
        P(),
        P(ROW, COL, None, None),
        P(ROW, COL),
        P(ROW, COL, None, None, None),
        P(by_row),
        P(by_row, None),
    )
    out_specs = (P(by_row, None), P(by_col, None), P(), P())
    return jax.shard_map(body, mesh=sub, in_specs=in_specs, out_specs=out_specs, check_vma=False)
```

```python
import jax
import jax.numpy as jnp
from jax import lax
from jax.experimental import pallas as pl
from jax.experimental.pallas import tpu as pltpu
from jax.sharding import Mesh, PartitionSpec as P

COL = ("z", "x")
ROW = ("y", "core")
VMEM = pl.BlockSpec(memory_space=pltpu.VMEM)
SMEM = pl.BlockSpec(memory_space=pltpu.SMEM)
F32 = jnp.float32
BF16 = jnp.bfloat16


UNROLL = 4


def forward_kernel(info, tiles, own, other, out, total):
    slots = tiles.shape[0]
    count = info[2 * slots]
    core = info[2 * slots + 1]
    n_x, n_z = out.shape[:2]
    total[...] = jnp.zeros_like(total)

    def step(b, _):
        places, products = [], []
        for u in range(UNROLL):
            k = b * UNROLL + u
            r = info[k]
            c = info[slots + k]
            half = c // 2
            picked = jnp.where((c % 2) == core, own[half], other[half])
            product = jnp.dot(tiles[k], picked, preferred_element_type=F32)
            products.append(jnp.where(k < count, product, 0.0))
            places.append(r % n_x * n_z + r // n_x)
        for place, product in zip(places, products):
            total[place] += product
        return 0

    lax.fori_loop(0, (count + UNROLL - 1) // UNROLL, step, 0)
    out[...] = total[...].reshape(out.shape).astype(out.dtype)


def backward_kernel(info, tiles, g0, g1, g2_low, g2_high, g3, keep, send, total):
    slots = tiles.shape[0]
    count = info[2 * slots]
    core = info[2 * slots + 1]
    here = info[2 * slots + 2]
    n_half = keep.shape[0]
    half_z = g2_low.shape[0]
    total[...] = jnp.zeros_like(total)

    def step(b, _):
        places, products = [], []
        for u in range(UNROLL):
            k = b * UNROLL + u
            r = info[k]
            c = info[slots + k]
            z = r // 4
            d = (r % 4 - here + 4) % 4
            far = jnp.where(z < half_z, g2_low[z % half_z], g2_high[z % half_z])
            picked = jnp.where(
                d < 2,
                jnp.where(d == 0, g0[z], g1[z]),
                jnp.where(d == 2, far, g3[z]),
            )
            product = lax.dot_general(
                tiles[k], picked, (((0,), (0,)), ((), ())), preferred_element_type=F32
            )
            products.append(jnp.where(k < count, product, 0.0))
            places.append(jnp.where((c % 2) == core, 0, n_half) + c // 2)
        for place, product in zip(places, products):
            total[place] += product
        return 0

    lax.fori_loop(0, (count + UNROLL - 1) // UNROLL, step, 0)
    keep[...] = total[:n_half]
    send[...] = total[n_half:].astype(send.dtype)


def ring(n, d):
    return [(i, (i + d) % n) for i in range(n)]


def repeat(a, n):
    return jnp.broadcast_to(a[None], (n,) + a.shape)


def body(
    features, col_norm, weight, bias, tile_coords, tile_count, tile_values, row_norm, cotangent
):
    n, hidden = features.shape
    n_y, n_core = lax.axis_size("y"), lax.axis_size("core")
    n_z, n_x = lax.axis_size("z"), lax.axis_size("x")
    tile_rows, tile_cols = n_z * n_x, n_y * n_core
    scale = float(n * tile_rows * tile_cols) ** (-0.5)
    tiles = tile_values[0, 0]
    coords = tile_coords[0, 0]
    swap = [(0, 1), (1, 0)]
    info = jnp.concatenate(
        [
            coords[:, 0],
            coords[:, 1],
            tile_count[0],
            lax.axis_index("core").reshape(1),
            lax.axis_index("x").reshape(1),
        ]
    )

    share = (col_norm[:, None] * features.astype(F32)).astype(BF16)
    own = lax.all_to_all(repeat(share, n_y), "y", 0, 0, tiled=True)
    other = lax.ppermute(own, "core", swap)

    blocks = pl.pallas_call(
        forward_kernel,
        out_shape=jax.ShapeDtypeStruct((n_x, n_z, n, hidden), BF16),
        in_specs=[SMEM, VMEM, VMEM, VMEM],
        out_specs=VMEM,
        scratch_shapes=[pltpu.VMEM((tile_rows, n, hidden), F32)],
        compiler_params=pltpu.CompilerParams(vmem_limit_bytes=40 * 2**20),
        name="forward_tiles",
    )(info, tiles, own, other)
    over_x = jnp.sum(lax.all_to_all(blocks, "x", 0, 0, tiled=True).astype(F32), axis=0)
    terms = lax.all_to_all(over_x.astype(BF16), "z", 0, 0, tiled=True)
    mixed = jnp.sum(terms.astype(F32), axis=0)

    high = mixed.astype(BF16)
    low = (mixed - high.astype(F32)).astype(BF16)
    rowsum = jnp.dot(high, weight, preferred_element_type=F32) + jnp.dot(
        low, weight, preferred_element_type=F32
    )
    pre = row_norm[:, None] * rowsum + bias[None, :]
    sigma = jax.nn.sigmoid(pre)
    output = (pre * sigma).astype(BF16)
    grad_pre = cotangent.astype(F32) * (sigma * (1.0 + pre * (1.0 - sigma)))
    grad_here = (grad_pre * row_norm[:, None]).astype(BF16)

    weight_part = lax.dot_general(
        high, grad_here, (((0,), (0,)), ((), ())), preferred_element_type=F32
    )
    bias_part = jnp.sum(grad_pre, axis=0)
    chunk = hidden // tile_cols
    both = jnp.concatenate(
        [
            (weight_part * scale).reshape(n_y, n_core * chunk, hidden),
            jnp.broadcast_to(bias_part * scale, (n_y, 8, hidden)),
        ],
        axis=1,
    ).astype(BF16)
    g0 = lax.all_to_all(repeat(grad_here, n_z), "z", 0, 0, tiled=True)
    g0, both = lax.optimization_barrier((g0, both))
    g1 = lax.ppermute(g0, "x", ring(n_x, n_x - 1))
    g3 = lax.ppermute(g0, "x", ring(n_x, 1))
    g2_low = lax.ppermute(g1[: n_z // 2], "x", ring(n_x, n_x - 1))
    g2_high = lax.ppermute(g3[n_z // 2 :], "x", ring(n_x, 1))
    g = [g0, g1, g2_low, g2_high, g3]
    both = jnp.sum(lax.all_to_all(both, "y", 0, 0, tiled=True).astype(F32), axis=0)
    first = lax.axis_index("core") == 0
    one, two, bias_sum = both[:chunk], both[chunk : 2 * chunk], both[2 * chunk :]
    mine = jnp.concatenate([jnp.where(first, one, two), bias_sum], axis=0)
    away = jnp.concatenate([jnp.where(first, two, one), bias_sum], axis=0).astype(BF16)
    both = mine + lax.ppermute(away, "core", swap).astype(F32)
    both = lax.all_to_all(repeat(both.astype(BF16), tile_rows), COL, 0, 0, tiled=True)
    both = jnp.sum(both.astype(F32), axis=0)
    grad_bias = both[chunk]
    chunk_here = both[:chunk].astype(BF16)

    keep, send = pl.pallas_call(
        backward_kernel,
        out_shape=(
            jax.ShapeDtypeStruct((n_y, n, hidden), F32),
            jax.ShapeDtypeStruct((n_y, n, hidden), BF16),
        ),
        in_specs=[SMEM] + [VMEM] * 6,
        out_specs=(VMEM, VMEM),
        scratch_shapes=[pltpu.VMEM((tile_cols, n, hidden), F32)],
        compiler_params=pltpu.CompilerParams(vmem_limit_bytes=40 * 2**20),
        name="backward_tiles",
    )(info, tiles, *g)
    pair = (keep + lax.ppermute(send, "core", swap).astype(F32)).astype(BF16)
    last = jnp.concatenate([pair, repeat(chunk_here, n_y)], axis=1)
    last = lax.all_to_all(last, "y", 0, 0, tiled=True)
    column_total = jnp.sum(last[:, :n].astype(F32), axis=0)
    chunks = last[:, n:]
    chunks_other = lax.ppermute(chunks, "core", swap)
    grad_weight = jnp.concatenate(
        [jnp.where(first, chunks, chunks_other), jnp.where(first, chunks_other, chunks)], axis=1
    )
    grad_weight = grad_weight.reshape(hidden, hidden).astype(F32)
    grad_mixed = (col_norm[:, None] * column_total).astype(BF16)
    grad_features = lax.dot_general(
        grad_mixed, weight, (((1,), (1,)), ((), ())), preferred_element_type=F32
    ).astype(BF16)
    return (output, grad_features, grad_weight, grad_bias)


def solution(mesh):
    devices = mesh.devices
    sub = Mesh(devices.reshape(8, 2, 8, 4), ("y", "core", "z", "x"))
    by_col = ("z", "x", "y", "core")
    by_row = ("y", "core", "z", "x")
    in_specs = (
        P(by_col, None),
        P(by_col),
        P(),
        P(),
        P(ROW, COL, None, None),
        P(ROW, COL),
        P(ROW, COL, None, None, None),
        P(by_row),
        P(by_row, None),
    )
    out_specs = (P(by_row, None), P(by_col, None), P(), P())
    return jax.shard_map(body, mesh=sub, in_specs=in_specs, out_specs=out_specs, check_vma=False)
```
